256 devices in a mesh: scan: 32 (over y, z_hi, core), cuts: 8 (over x, z_lo).
Axes of the slice: x: 4, y: 4, z: 8 (z_hi: 4, z_lo: 2; z = z_hi * 2 + z_lo), core: 2. Of those that a mesh axis runs over, the one named last changes fastest.
Arguments:
- positions: int32 [64, 2], P('scan'), may hold values from 0 to 768, as said below
- probe: float32 [2, 256, 256], replicated, may hold values from -5 to 5
- prop_phase: float32 [256, 256], replicated, may hold values from -3.140625 to 3.140625
- transmission: float32 [2, 16, 8192, 1024], P(None, 'cuts', 'scan'), may hold values from -1 to 1, as said below
- measured: float32 [64, 256, 256], P('scan'), may hold values from 0.05 to 2
Outputs:
- object_grad: float32 [2, 16, 8192, 1024], P(None, 'cuts', 'scan')
- probe_grad: float32 [2, 256, 256], P(None, 'cuts')
The draws below stay inside these ranges and needn't reach their ends.
Inputs may be any that keep to these rules, and one draw needn't show every extreme that they name: positions[p, 0] is the top row of position p's window within the tile of scan block p // 2 and lies below 256; positions[p, 1] is its left column, at most 768. In every block of 2 rows one row has top row 255 and another has left column 768. `transmission`: entries of modulus at most 1.
All inputs are finite; a program needn't handle non-finite values.
Results may differ from the reference program's by a relative error of at most 0.0003.
Values sent between devices are 32-bit elements; how exact they have to be, the bound alone decides.
No kernel may reach another device: no remote copies, remote signals or barrier semaphores. Data moves between devices by JAX's collectives and lax.ppermute only.
A program may use at most 128 MiB of HBM per device.

```python
import math
import jax
import jax.numpy as jnp
from jax import lax

PW = 256
TILE_R = 256
OBJ_C = 1024
POS_DEV = 2
SLICES = 16
NR = 8192
POSITIONS = 64


def draw_positions(key, part):
    key = jax.random.fold_in(key, 5)
    key_rows, key_cols, key_pick = jax.random.split(key, 3)
    row_offsets = jax.random.randint(key_rows, (POSITIONS,), 0, TILE_R)
    col_offsets = jax.random.randint(key_cols, (POSITIONS,), 0, OBJ_C - PW + 1)
    picks = jax.random.randint(key_pick, (POSITIONS // POS_DEV, 1), 0, POS_DEV)
    slot_index = jnp.arange(POS_DEV, dtype=jnp.int32)[None, :]
    row_force = (slot_index == picks).reshape(-1)
    col_force = (slot_index == (picks + 1) % POS_DEV).reshape(-1)
    row_offsets = jnp.where(row_force, TILE_R - 1, row_offsets)
    col_offsets = jnp.where(col_force, OBJ_C - PW, col_offsets)
    return jnp.stack([row_offsets, col_offsets], axis=1).astype(jnp.int32)


def draw_transmission(key, part):
    key = jax.random.fold_in(key, 11)
    key_amp, key_phase = jax.random.split(key)
    shape = (SLICES, NR, OBJ_C)
    amplitude = jax.random.uniform(key_amp, shape, jnp.float32, 0.95, 1.0)
    phase = 0.5 * jax.random.normal(key_phase, shape, jnp.float32)
    return jnp.stack([amplitude * jnp.cos(phase), amplitude * jnp.sin(phase)]).astype(jnp.float32)


def level_of(stream_key, shape, cuts, low, high):
    level, own = 1.0, jax.random.fold_in(stream_key, 6)
    for position, parts in cuts:
        steps = jnp.exp(jax.random.uniform(jax.random.fold_in(own, position), (parts,), jnp.float32, low / len(cuts), high / len(cuts)))
        level = level * jnp.repeat(steps, shape[position] // parts).reshape([-1 if axis == position else 1 for axis in range(len(shape))])
    return level


def scatter_about(key, shape, deviation, bound, held_as=jnp.bfloat16):
    return jnp.clip(deviation * jax.random.normal(key, shape, jnp.float32), -bound, bound).astype(held_as)


def setup_inputs(seed: int = 0) -> dict:
    streams_of = jax.random.split(jax.random.key(seed), 6)
    return {
        "positions": draw_positions(jax.random.fold_in(streams_of[5], 71), 0),
        "probe": scatter_about(streams_of[1], (2, PW, PW), 1.0, 5.0, jnp.float32),
        "prop_phase": jnp.clip(jax.random.uniform(streams_of[2], (PW, PW), jnp.float32, -3.140625, 3.140625), -3.140625, 3.140625),
        "transmission": draw_transmission(jax.random.fold_in(streams_of[5], 71), 0),
        "measured": jnp.clip(jnp.exp(math.log(2.0) - 3.6888794 * jax.random.uniform(streams_of[4], (POSITIONS, PW, PW), jnp.float32) ** level_of(streams_of[4], (POSITIONS, PW, PW), ((0, 32),), -0.2, 0.2)), 0.05, 2.0),
    }


def forward_two(field):
    return jnp.fft.fft2(field, norm="ortho")


def inverse_two(field):
    return jnp.fft.ifft2(field, norm="ortho")


def reference(positions, probe, prop_phase, transmission, measured):
    extent = probe.shape[1]
    total_rows = transmission.shape[2]
    depth = transmission.shape[1]
    obj_field = transmission[0] + 1j * transmission[1]
    extended = jnp.concatenate([obj_field, obj_field[:, :extent]], axis=1)
    kernel = jnp.cos(prop_phase) + 1j * jnp.sin(prop_phase)
    entry = probe[0] + 1j * probe[1]
    owners = jnp.arange(positions.shape[0], dtype=jnp.int32) // POS_DEV
    tops = (owners * TILE_R + positions[:, 0]).astype(jnp.int32)
    lefts = positions[:, 1].astype(jnp.int32)

    def visit(carry, item):
        grad_field, probe_acc = carry
        top_row, left_col, target = item
        patches = [lax.dynamic_slice(extended[layer_no], (top_row, left_col), (extent, extent)) for layer_no in range(depth)]
        history = []
        wavefield = entry
        spectrum = entry
        for layer_no in range(depth):
            history.append(wavefield)
            spectrum = forward_two(patches[layer_no] * wavefield)
            if layer_no < depth - 1:
                wavefield = inverse_two(kernel * spectrum)
        power = spectrum.real * spectrum.real + spectrum.imag * spectrum.imag
        chi_grad = inverse_two((power - target) * spectrum)
        grad_wave = chi_grad
        for layer_no in reversed(range(depth)):
            if layer_no < depth - 1:
                chi_grad = inverse_two(jnp.conj(kernel) * forward_two(grad_wave))
            piece = jnp.conj(history[layer_no]) * chi_grad
            spot = (jnp.int32(layer_no), top_row, left_col)
            region = lax.dynamic_slice(grad_field, spot, (1, extent, extent))
            grad_field = lax.dynamic_update_slice(grad_field, region + piece[None], spot)
            grad_wave = jnp.conj(patches[layer_no]) * chi_grad
        return (grad_field, probe_acc + grad_wave), None

    start_state = (jnp.zeros(extended.shape, extended.dtype), jnp.zeros(entry.shape, entry.dtype))
    final_state, unused = lax.scan(visit, start_state, (tops, lefts, measured))
    grad_field, probe_acc = final_state
    folded = grad_field[:, :total_rows].at[:, :extent].add(grad_field[:, total_rows:])
    object_grad = jnp.stack([folded.real, folded.imag]).astype(jnp.float32)
    probe_grad = jnp.stack([probe_acc.real, probe_acc.imag]).astype(jnp.float32)
    return object_grad, probe_grad
```

```python
import math

import jax
import jax.numpy as jnp
import ml_dtypes
import numpy as np
from jax import lax
from jax.experimental import pallas as pl
from jax.experimental.pallas import tpu as pltpu
from jax.sharding import PartitionSpec as P


AXES = ("scan", "cuts")
N = 256
H = 128
BF = jnp.bfloat16
F32 = jnp.float32


def dft_constants():
    k = np.arange(H)[:, None].astype(np.float64)
    j = np.arange(H)[None, :].astype(np.float64)
    even = np.exp(-2j * np.pi * j * k / H) / math.sqrt(N)
    odd = np.exp(-2j * np.pi * j * (2 * k + 1) / N) / math.sqrt(N)

    def real_form(c):
        return np.block([[c.real, -c.imag], [c.imag, c.real]])

    def parts(m):
        hi = m.astype(np.float32).astype(ml_dtypes.bfloat16)
        lo = (m - hi.astype(np.float64)).astype(np.float32).astype(ml_dtypes.bfloat16)
        return hi, hi, lo

    def wide(m):
        return np.concatenate(parts(m), axis=1)

    def tall(m):
        return np.concatenate(parts(m), axis=0)

    e, o = real_form(even), real_form(odd)
    left = np.stack([wide(e), wide(o), wide(e.T), wide(o.T)])
    right = np.stack([tall(e.T), tall(o.T), tall(e), tall(o)])
    return left, right


def split(x):
    hi = x.astype(BF)
    lo = (x - hi.astype(F32)).astype(BF)
    return hi, lo


def left_dot(m, x):
    hi, lo = split(x)
    return jnp.dot(m, jnp.concatenate([hi, lo, hi], axis=0), preferred_element_type=F32)


def right_dot(x, m):
    hi, lo = split(x)
    return jnp.dot(jnp.concatenate([hi, lo, hi], axis=1), m, preferred_element_type=F32)


def cat0(a, b):
    return jnp.concatenate([a, b], axis=0)


def cat1(a, b):
    return jnp.concatenate([a, b], axis=1)


def dft(re, im, lm, rm):
    u = cat0(re[:H] + re[H:], im[:H] + im[H:])
    v = cat0(re[:H] - re[H:], im[:H] - im[H:])
    ye = left_dot(lm[0], u)
    yo = left_dot(lm[1], v)

    def cols(y):
        r, i = y[:H], y[H:]
        return (
            cat1(r[:, :H] + r[:, H:], i[:, :H] + i[:, H:]),
            cat1(r[:, :H] - r[:, H:], i[:, :H] - i[:, H:]),
        )

    ue, ve = cols(ye)
    uo, vo = cols(yo)
    return right_dot(cat0(ue, uo), rm[0]), right_dot(cat0(ve, vo), rm[1])


def idft(pe, po, lm, rm):
    e = right_dot(pe, rm[2])
    o = right_dot(po, rm[3])
    lt, rt = e + o, e - o
    re = cat1(lt[:, :H], rt[:, :H])
    im = cat1(lt[:, H:], rt[:, H:])
    a = left_dot(lm[2], cat0(re[:H], im[:H]))
    b = left_dot(lm[3], cat0(re[H:], im[H:]))
    t, w = a + b, a - b
    return cat0(t[:H], w[:H]), cat0(t[H:], w[H:])


def times_kernel(p, kr, ki, sign):
    r, i = p[:, :H], p[:, H:]
    if sign > 0:
        return cat1(r * kr - i * ki, r * ki + i * kr)
    return cat1(r * kr + i * ki, i * kr - r * ki)


def chain_body(meta, probe_in, lm, rm, kr, ki, target, own, k1, k2, k3, g1, g2, g3,
               pieces, probe_out, w, hist, psi, out, in_sem, out_sem):
    hubx, plane, active = meta[0], meta[1], meta[2]

    def propagate(re, im, sign):
        pe, po = dft(re, im, lm, rm)
        return idft(times_kernel(pe, kr[0], ki[0], sign), times_kernel(po, kr[1], ki[1], sign), lm, rm)

    @pl.when(active == 1)
    def _():
        sources = [(0, own, None), (1, k1, g1), (2, k2, g2), (3, k3, g3)]
        copies = []
        for d, keep, got in sources:
            x = lax.rem(hubx + d, 4)
            for which in range(2):
                s = 4 * x + 2 * (plane if which == 0 else 1 - plane)
                src = keep.at[which] if d == 0 else (keep if which == 0 else got)
                c = pltpu.make_async_copy(src, w.at[pl.ds(s, 2)], in_sem.at[2 * d + which])
                c.start()
                copies.append(c)
        for c in copies:
            c.wait()
        psi[...] = probe_in[...]

        def chi_of(s):
            wr, wi, pr, pi = w[s, 0], w[s, 1], psi[0], psi[1]
            return wr * pr - wi * pi, wr * pi + wi * pr

        def forward(s, c):
            hist[s] = psi[...]
            re, im = chi_of(s)
            re, im = propagate(re, im, 1)
            psi[0] = re
            psi[1] = im
            return c

        lax.fori_loop(0, 15, forward, 0)
        re, im = chi_of(15)
        pe, po = dft(re, im, lm, rm)

        def detect(p, m):
            r, i = p[:, :H], p[:, H:]
            f = r * r + i * i - m
            return cat1(r * f, i * f)

        re, im = idft(detect(pe, target[0]), detect(po, target[1]), lm, rm)

        def emit(s, gr, gi, pr, pi):
            out[s, 0] = pr * gr + pi * gi
            out[s, 1] = pr * gi - pi * gr
            wr, wi = w[s, 0], w[s, 1]
            return wr * gr + wi * gi, wr * gi - wi * gr

        nr, ni = emit(15, re, im, psi[0], psi[1])
        psi[0] = nr
        psi[1] = ni

        def backward(q, c):
            s = 14 - q
            re, im = propagate(psi[0], psi[1], -1)
            nr, ni = emit(s, re, im, hist[s, 0], hist[s, 1])
            psi[0] = nr
            psi[1] = ni
            return c

        lax.fori_loop(0, 15, backward, 0)
        probe_out[...] = psi[...]
        outs = []
        for d in range(4):
            x = lax.rem(hubx + d, 4)
            for which in range(2):
                s = 4 * x + 2 * (plane if which == 0 else 1 - plane)
                c = pltpu.make_async_copy(
                    out.at[pl.ds(s, 2)], pieces.at[d, which], out_sem.at[2 * d + which]
                )
                c.start()
                outs.append(c)
        for c in outs:
            c.wait()

    @pl.when(active == 0)
    def _():
        probe_out[...] = jnp.zeros_like(probe_out)


def run_chain(meta, probe_in, lm, rm, kr, ki, target, own, k1, k2, k3, g1, g2, g3):
    vm = pl.BlockSpec(memory_space=pltpu.VMEM)
    hbm = pl.BlockSpec(memory_space=pl.ANY)
    return pl.pallas_call(
        chain_body,
        out_shape=(
            jax.ShapeDtypeStruct((4, 2, 2, 2, N, N), F32),
            jax.ShapeDtypeStruct((2, N, N), F32),
        ),
        in_specs=[pl.BlockSpec(memory_space=pltpu.SMEM)] + [vm] * 6 + [hbm] * 7,
        out_specs=(hbm, vm),
        scratch_shapes=[
            pltpu.VMEM((16, 2, N, N), F32),
            pltpu.VMEM((15, 2, N, N), F32),
            pltpu.VMEM((2, N, N), F32),
            pltpu.VMEM((16, 2, N, N), F32),
            pltpu.SemaphoreType.DMA((8,)),
            pltpu.SemaphoreType.DMA((8,)),
        ],
        compiler_params=pltpu.CompilerParams(vmem_limit_bytes=56 * 1024 * 1024),
    )(meta, probe_in, lm, rm, kr, ki, target, own, k1, k2, k3, g1, g2, g3)


def spectral(x):
    return x.reshape(H, 2, H, 2).transpose(3, 1, 0, 2).reshape(2, N, H)


def shards(positions, probe, prop_phase, transmission, measured):
    scan_count = lax.axis_size("scan")
    cut_count = lax.axis_size("cuts")
    scan = lax.axis_index("scan")
    cut = lax.axis_index("cuts")
    core = scan % 2
    x, z = cut // 2, cut % 2
    hubx = jnp.where(core == 0, 0, 2)
    is_hub = x == hubx

    def send(value, route, where=lambda t, c: True):
        pairs = []
        for t in range(scan_count):
            for c in range(cut_count):
                if where(t, c):
                    tt, cc = route(t, c)
                    pairs.append((t * cut_count + c, (tt % scan_count) * cut_count + cc))
        return lax.ppermute(value, AXES, pairs)

    def hub_of(t):
        return 0 if t % 2 == 0 else 2

    def to_hub(value, d):
        return send(
            value,
            lambda t, c: (t, 2 * hub_of(t) + c % 2),
            lambda t, c: c // 2 == (hub_of(t) + d) % 4,
        )

    def from_hub(value, d):
        return send(
            value,
            lambda t, c: (t, 2 * ((hub_of(t) + d) % 4) + c % 2),
            lambda t, c: c // 2 == hub_of(t),
        )

    def swap_planes(value):
        return send(value, lambda t, c: (t, c ^ 1))

    def next_tile(value):
        return send(value, lambda t, c: (t + 1, c))

    def previous_tile(value):
        return send(value, lambda t, c: (t - 1, c))

    first_is_a = (positions[0, 0] == N - 1) & (positions[1, 1] == 768)
    a_index = jnp.where(first_is_a, 0, 1)
    b_index = 1 - a_index
    left_own = positions[a_index, 1]
    top_b = positions[b_index, 0]

    field = transmission.transpose(1, 0, 2, 3)
    last_row = field[:, :, N - 1 :, :]
    packed = jnp.concatenate(
        [last_row.reshape(-1), jnp.full((128,), left_own.astype(F32))]
    )
    packed_prev = next_tile(packed)
    row_prev = packed_prev[:4096].reshape(2, 2, 1, 1024)
    left_a = packed_prev[4096].astype(jnp.int32)
    target_a = send(
        measured[a_index], lambda t, c: (t + 1, c), lambda t, c: c == 2 * hub_of(t + 1)
    )
    rim = previous_tile(field[:, :, :, 768:])

    rows = lax.broadcasted_iota(jnp.int32, (N, N), 0)
    columns = lax.broadcasted_iota(jnp.int32, (N, N), 1)

    block_a = left_a // N
    shift_a = left_a % N
    block_a2 = jnp.minimum(block_a + 1, 3)

    def pick(array):
        size = array.shape[:3] + (N,)
        one = lax.dynamic_slice(array, (0, 0, 0, block_a * N), size)
        two = lax.dynamic_slice(array, (0, 0, 0, block_a2 * N), size)
        return jnp.where(columns[: size[2]] >= shift_a, one, two)

    window_a = jnp.where(rows == N - 1, pick(row_prev), pick(field))
    window_b = jnp.where(rows >= top_b, field[:, :, :, 768:], rim)
    keep = jnp.where(z == 0, window_a, window_b)
    give = jnp.where(z == 0, window_b, window_a)
    k = [to_hub(keep, d) for d in (1, 2, 3)]
    got = swap_planes(give)
    g = [to_hub(got, d) for d in (1, 2, 3)]

    roll_row = jnp.where(z == 0, N - 1, top_b)
    roll_col = jnp.where(z == 0, shift_a, 0)
    probe_in = jnp.roll(probe, (roll_row, roll_col), (1, 2))
    phase = spectral(prop_phase)
    target = spectral(jnp.where(z == 0, target_a, measured[b_index]))
    left, right = dft_constants()
    meta = jnp.stack([hubx, z, is_hub.astype(jnp.int32)]).astype(jnp.int32)
    pieces, probe_part = run_chain(
        meta, probe_in, jnp.asarray(left), jnp.asarray(right), jnp.cos(phase), jnp.sin(phase),
        target, jnp.stack([keep, got]), *k, *g,
    )
    probe_part = jnp.roll(probe_part, (-roll_row, -roll_col), (1, 2))

    spread = lax.all_to_all(probe_part, "cuts", 1, 1, tiled=True)
    own_rows = N // cut_count
    total = jnp.sum(spread.reshape(2, cut_count, own_rows, N), axis=1)
    total = total + send(total, lambda t, c: (t ^ 1, c))
    for stride in (2, 8):
        base = [
            send(
                total,
                lambda t, c: (t - (t // stride % 4) * stride + ((t // stride % 4 + turn) % 4) * stride, c),
            )
            for turn in (1, 2, 3)
        ]
        total = total + base[0] + base[1] + base[2]
    probe_grad = total

    back = [from_hub(pieces[d], d) for d in (1, 2, 3)]
    mine = jnp.where(is_hub, pieces[0], 0.0) + back[0] + back[1] + back[2]
    kept = mine[0]
    swapped = swap_planes(mine[1])
    grad_a = jnp.where(z == 0, kept, swapped)
    grad_b = jnp.where(z == 0, swapped, kept)
    low_b = next_tile(jnp.where(rows < top_b, grad_b, 0.0))
    top_row = previous_tile(grad_a[:, :, N - 1 :, :])

    block_own = left_own // N
    shift_own = left_own % N

    def place(value, block, shift, index):
        cols = columns[: value.shape[2]]
        return jnp.where((block == index) & (cols >= shift), value, 0.0) + jnp.where(
            (block + 1 == index) & (cols < shift), value, 0.0
        )

    parts = []
    for index in range(4):
        part = jnp.where(rows < N - 1, place(grad_a, block_a, shift_a, index), 0.0)
        extra = jnp.broadcast_to(place(top_row, block_own, shift_own, index), part.shape)
        part = part + jnp.where(rows == N - 1, extra, 0.0)
        if index == 3:
            part = part + jnp.where(rows >= top_b, grad_b, 0.0) + low_b
        parts.append(part)
    object_grad = jnp.concatenate(parts, axis=3).transpose(1, 0, 2, 3)
    return object_grad, probe_grad


def solution(mesh):
    in_specs = (P("scan", None), P(), P(), P(None, "cuts", "scan", None), P("scan", None, None))
    out_specs = (P(None, "cuts", "scan", None), P(None, "cuts", None))
    return jax.shard_map(shards, mesh=mesh, in_specs=in_specs, out_specs=out_specs, check_vma=False)
```

```python
import math

import jax
import jax.numpy as jnp
import ml_dtypes
import numpy as np
from jax import lax
from jax.experimental import pallas as pl
from jax.experimental.pallas import tpu as pltpu
from jax.sharding import PartitionSpec as P


AXES = ("scan", "cuts")
N = 256
H = 128
BF = jnp.bfloat16
F32 = jnp.float32


def dft_constants():
    k = np.arange(H)[:, None].astype(np.float64)
    j = np.arange(H)[None, :].astype(np.float64)
    even = np.exp(-2j * np.pi * j * k / H) / math.sqrt(N)
    odd = np.exp(-2j * np.pi * j * (2 * k + 1) / N) / math.sqrt(N)

    def real_form(c):
        return np.block([[c.real, -c.imag], [c.imag, c.real]])

    def parts(m):
        hi = m.astype(np.float32).astype(ml_dtypes.bfloat16)
        lo = (m - hi.astype(np.float64)).astype(np.float32).astype(ml_dtypes.bfloat16)
        return hi, lo

    e, o = real_form(even), real_form(odd)
    tables = [parts(m) for m in (e, o, e.T, o.T)]
    order = np.zeros((N, N), np.float32)
    order[np.arange(N), np.concatenate([np.arange(0, N, 2), np.arange(1, N, 2)])] = 1.0
    return np.stack([np.stack(t) for t in tables]), order


def split(x):
    hi = x.astype(BF)
    lo = (x - hi.astype(F32)).astype(BF)
    return hi, lo


def left_dot(mats, index, x):
    hi, lo = split(x)
    m = jnp.concatenate([mats[index, 0], mats[index, 0], mats[index, 1]], axis=1)
    return jnp.dot(m, jnp.concatenate([hi, lo, hi], axis=0), preferred_element_type=F32)


def right_dot(x, mats, index):
    hi, lo = split(x)
    m = jnp.concatenate([mats[index, 0], mats[index, 0], mats[index, 1]], axis=0)
    return jnp.dot(jnp.concatenate([hi, lo, hi], axis=1), m, preferred_element_type=F32)


def cat0(a, b):
    return jnp.concatenate([a, b], axis=0)


def cat1(a, b):
    return jnp.concatenate([a, b], axis=1)


def dft(re, im, mats):
    u = cat0(re[:H] + re[H:], im[:H] + im[H:])
    v = cat0(re[:H] - re[H:], im[:H] - im[H:])
    ye = left_dot(mats, 0, u)
    yo = left_dot(mats, 1, v)

    def cols(y):
        r, i = y[:H], y[H:]
        return (
            cat1(r[:, :H] + r[:, H:], i[:, :H] + i[:, H:]),
            cat1(r[:, :H] - r[:, H:], i[:, :H] - i[:, H:]),
        )

    ue, ve = cols(ye)
    uo, vo = cols(yo)
    return right_dot(cat0(ue, uo), mats, 2), right_dot(cat0(ve, vo), mats, 3)


def idft(pe, po, mats):
    e = right_dot(pe, mats, 0)
    o = right_dot(po, mats, 1)
    lt, rt = e + o, e - o
    re = cat1(lt[:, :H], rt[:, :H])
    im = cat1(lt[:, H:], rt[:, H:])
    a = left_dot(mats, 2, cat0(re[:H], im[:H]))
    b = left_dot(mats, 3, cat0(re[H:], im[H:]))
    t, w = a + b, a - b
    return cat0(t[:H], w[:H]), cat0(t[H:], w[H:])


def times_kernel(p, kr, ki, sign):
    r, i = p[:, :H], p[:, H:]
    if sign > 0:
        return cat1(r * kr - i * ki, r * ki + i * kr)
    return cat1(r * kr + i * ki, i * kr - r * ki)


BLOCK = 4 * N


def chain_body(forward, backward, meta, *refs):
    refs = list(refs)
    fixed = [refs.pop(0) for _ in range(5 if forward and backward else 4)]
    windows = [refs.pop(0) for _ in range(8)]
    old = refs.pop(0) if not forward else None
    if not forward:
        refs = refs[4:]
    wave_out = refs.pop(0)
    past_out = refs.pop(0) if not backward else None
    pieces = [refs.pop(0) for _ in range(4)] if backward else None
    w, hist, psi, out, wave_in, mats, kr, ki, target, in_sem, past_sem, out_sem, fixed_sem = refs
    plane, block, row, col = meta[0], meta[1], meta[2], meta[3]
    active = meta[5] if forward and backward else meta[4]
    slots = [
        4 * b + 2 * s + layer
        for b, s in (
            (block, plane), (block, 1 - plane), (1 - block, plane), (1 - block, 1 - plane)
        )
        for layer in range(2)
    ]

    def propagate(re, im, sign):
        pe, po = dft(re, im, mats)
        pe = times_kernel(pe, kr[:, :H], ki[:, :H], sign)
        po = times_kernel(po, kr[:, H:], ki[:, H:], sign)
        return idft(pe, po, mats)

    def past_copy(s):
        if forward:
            return pltpu.make_async_copy(hist.at[s], past_out.at[s], past_sem.at[s])
        return pltpu.make_async_copy(old.at[s], hist.at[s], past_sem.at[s])

    def wait_window(s):
        pltpu.make_async_copy(windows[0], w.at[s], in_sem.at[s]).wait()

    @pl.when(active == 1)
    def _():
        for i in range(8):
            pltpu.make_async_copy(windows[i], w.at[slots[i]], in_sem.at[slots[i]]).start()
        if not forward:
            for s in range(7, -1, -1):
                past_copy(s).start()
        for i, (source, place) in enumerate(zip(fixed, (wave_in, mats, kr, ki, target))):
            pltpu.make_async_copy(source, place, fixed_sem.at[i]).start()
        for i, (source, place) in enumerate(zip(fixed, (wave_in, mats, kr, ki, target))):
            pltpu.make_async_copy(source, place, fixed_sem.at[i]).wait()
        if forward and not backward:
            for part in range(2):
                psi[part] = pltpu.roll(pltpu.roll(wave_in[part], row, 0), col, 1)
        else:
            psi[...] = wave_in[...]

        def chi_of(s):
            wr, wi, pr, pi = w[s, 0], w[s, 1], psi[0], psi[1]
            return wr * pr - wi * pi, wr * pi + wi * pr

        def step(s, c):
            wait_window(s)
            hist[s] = psi[...]
            re, im = chi_of(s)
            re, im = propagate(re, im, 1)
            psi[0] = re
            psi[1] = im
            return c

        def emit(s, gr, gi):
            pr, pi = hist[s, 0], hist[s, 1]
            out[s, 0] = pr * gr + pi * gi
            out[s, 1] = pr * gi - pi * gr
            wr, wi = w[s, 0], w[s, 1]
            psi[0] = wr * gr + wi * gi
            psi[1] = wr * gi - wi * gr

        def piece_copy(s, i, part):
            span = pl.ds((i % 2 * 2 + part) * N, N)
            return pltpu.make_async_copy(
                out.at[s, part], pieces[i // 2].at[span], out_sem.at[2 * i + part]
            )

        def leave(s):
            for i in range(8):

                @pl.when(s == slots[i])
                def _():
                    for part in range(2):
                        piece_copy(s, i, part).start()

        def step_back(count):
            def run(q, c):
                s = count - 1 - q
                if not forward:
                    wait_window(s)
                    past_copy(s).wait()

                re, im = propagate(psi[0], psi[1], -1)
                emit(s, re, im)
                leave(s)
                return c

            return run

        if forward and not backward:

            def run(s, c):
                step(s, c)
                past_copy(s).start()
                return c

            lax.fori_loop(0, 8, run, 0)
            wave_out[...] = psi[...]
            for s in range(8):
                past_copy(s).wait()
        if forward and backward:
            lax.fori_loop(0, 7, step, 0)
            wait_window(7)
            hist[7] = psi[...]
            re, im = chi_of(7)
            pe, po = dft(re, im, mats)

            def detect(p, m):
                r, i = p[:, :H], p[:, H:]
                f = r * r + i * i - m
                return cat1(r * f, i * f)

            re, im = idft(detect(pe, target[:, :H]), detect(po, target[:, H:]), mats)
            emit(7, re, im)
            leave(7)
            lax.fori_loop(0, 7, step_back(7), 0)
            wave_out[...] = psi[...]
        if backward and not forward:
            lax.fori_loop(0, 8, step_back(8), 0)
            for part in range(2):
                undone = pltpu.roll(psi[part], lax.rem(N - row, N), 0)
                wave_out[part] = pltpu.roll(undone, lax.rem(N - col, N), 1)
        if backward:
            for i in range(8):
                for part in range(2):
                    piece_copy(0, i, part).wait()

    if not forward:

        @pl.when(active == 0)
        def _():
            wave_out[...] = jnp.zeros_like(wave_out)


def run_chain(forward, backward, meta, wave, tables, target, windows, old, pieces):
    vm = pl.BlockSpec(memory_space=pltpu.VMEM)
    hbm = pl.BlockSpec(memory_space=pl.ANY)
    far = pl.BlockSpec(memory_space=pltpu.HBM)
    operands, specs = [meta, wave, *tables], [pl.BlockSpec(memory_space=pltpu.SMEM)] + [hbm] * 4
    if forward and backward:
        operands, specs = operands + [target], specs + [hbm]
    operands, specs = operands + list(windows), specs + [hbm] * 8
    aliases = {}
    if not forward:
        operands, specs = operands + [old, *pieces], specs + [far] * 5
        aliases = {len(operands) - 4 + i: 1 + i for i in range(4)}
    shapes, outs = [jax.ShapeDtypeStruct((2, N, N), F32)], [vm]
    if not backward:
        shapes, outs = shapes + [jax.ShapeDtypeStruct((8, 2, N, N), F32)], outs + [far]
    else:
        shapes += [jax.ShapeDtypeStruct((BLOCK, N), F32)] * 4
        outs = outs + [far] * 4
    return pl.pallas_call(
        lambda *refs: chain_body(forward, backward, *refs),
        out_shape=tuple(shapes),
        in_specs=specs,
        out_specs=tuple(outs),
        input_output_aliases=aliases,
        scratch_shapes=[
            pltpu.VMEM((8, 2, N, N), F32),
            pltpu.VMEM((8, 2, N, N), F32),
            pltpu.VMEM((2, N, N), F32),
            pltpu.VMEM((8, 2, N, N), F32),
            pltpu.VMEM((2, N, N), F32),
            pltpu.VMEM((4, 2, N, N), BF),
            pltpu.VMEM((N, N), F32),
            pltpu.VMEM((N, N), F32),
            pltpu.VMEM((N, N), F32),
            pltpu.SemaphoreType.DMA((8,)),
            pltpu.SemaphoreType.DMA((8,)),
            pltpu.SemaphoreType.DMA((16,)),
            pltpu.SemaphoreType.DMA((5,)),
        ],
        compiler_params=pltpu.CompilerParams(vmem_limit_bytes=22 * 1024 * 1024),
        cost_estimate=pl.CostEstimate(
            flops=10_000_000, bytes_accessed=1024 * 1024, transcendentals=0
        ),
    )(*operands)


def shards(positions, probe, prop_phase, transmission, measured):
    scan_count = lax.axis_size("scan")
    cut_count = lax.axis_size("cuts")
    scan = lax.axis_index("scan")
    cut = lax.axis_index("cuts")
    core = scan % 2
    x, z = cut // 2, cut % 2
    half = x // 2
    hubx = jnp.where(core == 0, 1 + half, 3 * half)
    is_hub = x == hubx

    def send(value, route, where=lambda t, c: True):
        pairs = []
        for t in range(scan_count):
            for c in range(cut_count):
                if where(t, c):
                    tt, cc = route(t, c)
                    pairs.append((t * cut_count + c, (tt % scan_count) * cut_count + cc))
        return lax.ppermute(value, AXES, pairs)

    def hub_of(t, h):
        return 1 + h if t % 2 == 0 else 3 * h

    def beside(t, c):
        return t, c ^ 1

    def along(t, c):
        return t, c ^ 2

    def across(t, c):
        return t, c ^ 3

    def at_hub(t, c):
        return c // 2 == hub_of(t, c // 4)

    def off_hub(t, c):
        return not at_hub(t, c)

    def to_other_half(t, c):
        return t, 2 * hub_of(t, 1 - c // 4) + c % 2

    def next_tile(value):
        return send(value, lambda t, c: (t + 1, c))

    def previous_tile(value):
        return send(value, lambda t, c: (t - 1, c))

    edge = [transmission[:, layer, :, 768:] for layer in range(2)]
    rim = [previous_tile(part) for part in edge]
    positions, edge = lax.optimization_barrier((positions, edge))

    first_is_a = (positions[0, 0] == N - 1) & (positions[1, 1] == 768)
    a_index = jnp.where(first_is_a, 0, 1)
    b_index = 1 - a_index
    left_own = positions[a_index, 1]
    top_b = positions[b_index, 0]

    rows = lax.broadcasted_iota(jnp.int32, (N, N), 0)
    columns = lax.broadcasted_iota(jnp.int32, (N, N), 1)

    packed = jnp.concatenate(
        [transmission[:, :, N - 1, :].reshape(-1), jnp.full((128,), left_own.astype(F32))]
    )
    packed_prev = next_tile(packed)
    row_prev = packed_prev[:4096].reshape(2, 2, 1, 1024)
    left_a = packed_prev[4096].astype(jnp.int32)
    target_a = send(
        measured[a_index], lambda t, c: (t + 1, c), lambda t, c: c == 2 * hub_of(t + 1, 1)
    )

    block_a = left_a // N
    shift_a = left_a % N
    block_a2 = jnp.minimum(block_a + 1, 3)

    def pick(array, layer):
        size = (2, 1, array.shape[2], N)
        one = lax.dynamic_slice(array, (0, layer, 0, block_a * N), size)
        two = lax.dynamic_slice(array, (0, layer, 0, block_a2 * N), size)
        return jnp.where(columns[: size[2]] >= shift_a, one, two)[:, 0]

    window_a = [
        jnp.where(rows == N - 1, pick(row_prev, layer), pick(transmission, layer))
        for layer in range(2)
    ]
    roll_row = jnp.where(z == 0, N - 1, top_b)
    roll_col = jnp.where(z == 0, shift_a, 0)
    mats, order = dft_constants()

    def spectral(value):
        value = jnp.dot(order, value, precision=lax.Precision.HIGHEST)
        return jnp.dot(value, order.T, precision=lax.Precision.HIGHEST)

    phase = spectral(prop_phase)
    target = spectral(jnp.where(z == 0, target_a, measured[b_index]))
    tables = (jnp.asarray(mats), jnp.cos(phase), jnp.sin(phase))
    meta = jnp.stack(
        [z, hubx % 2, roll_row, roll_col, is_hub & (half == 0), is_hub & (half == 1)]
    ).astype(jnp.int32)

    rim[0], window_a, target, tables = lax.optimization_barrier(
        (rim[0], window_a, target, tables)
    )
    windows = [[], [], [], []]
    for layer in range(2):
        window_b = jnp.where(rows >= top_b, edge[layer], rim[layer])
        keep = jnp.where(z == 0, window_a[layer], window_b)
        give = jnp.where(z == 0, window_b, window_a[layer])
        windows[0].append(keep)
        windows[1].append(send(give, beside, at_hub))
        windows[2].append(send(keep, along, off_hub))
        windows[3].append(send(give, across, off_hub))
    windows = sum(windows, [])
    wave, past = run_chain(True, False, meta, probe, tables, None, windows, None, None)
    wave = send(wave, to_other_half, lambda t, c: c < 4 and at_hub(t, c))
    wave, *pieces = run_chain(True, True, meta, wave, tables, target, windows, None, None)
    wave = send(wave, to_other_half, lambda t, c: c >= 4 and at_hub(t, c))
    wave, *pieces = run_chain(False, True, meta, wave, tables, None, windows, past, pieces)

    spread = lax.all_to_all(wave, "cuts", 1, 1, tiled=True)
    own_rows = N // cut_count
    total = jnp.sum(spread.reshape(2, cut_count, own_rows, N), axis=1)
    total = total + send(total, lambda t, c: (t ^ 1, c))
    for stride in (2, 8):

        def turned(t, turn):
            digit = t // stride % 4
            return t + ((digit + turn) % 4 - digit) * stride

        turns = [send(total, lambda t, c: (turned(t, turn), c)) for turn in (1, 2, 3)]
        total = total + turns[0] + turns[1] + turns[2]
    probe_grad = total

    lent = send(pieces[1], beside, at_hub)
    kept_far = send(pieces[2], along, at_hub)
    lent_far = send(pieces[3], across, at_hub)
    kept = jnp.where(is_hub, pieces[0], kept_far).reshape(2, 2, N, N)
    lent = jnp.where(is_hub, lent, lent_far).reshape(2, 2, N, N)
    grad_a = jnp.where(z == 0, kept, lent)
    grad_b = jnp.where(z == 0, lent, kept)
    low_b = next_tile(jnp.where(rows < top_b, grad_b, 0.0))
    top_row = previous_tile(grad_a[:, :, N - 1 :])

    block_own = left_own // N
    shift_own = left_own % N

    def place(value, block, shift, index):
        cols = columns[: value.shape[1]]
        return jnp.where((block == index) & (cols >= shift), value, 0.0) + jnp.where(
            (block + 1 == index) & (cols < shift), value, 0.0
        )

    whole = []
    for layer in range(2):
        parts = []
        for index in range(4):
            part = jnp.where(rows < N - 1, place(grad_a[layer], block_a, shift_a, index), 0.0)
            extra = place(top_row[layer], block_own, shift_own, index)
            part = part + jnp.where(rows == N - 1, extra, 0.0)
            if index == 3:
                part = part + jnp.where(rows >= top_b, grad_b[layer], 0.0) + low_b[layer]
            parts.append(part)
        whole.append(jnp.concatenate(parts, axis=2))
    object_grad = jnp.stack(whole, axis=1)
    return object_grad, probe_grad


def solution(mesh):
    in_specs = (P("scan", None), P(), P(), P(None, "cuts", "scan", None), P("scan", None, None))
    out_specs = (P(None, "cuts", "scan", None), P(None, "cuts", None))
    return jax.shard_map(shards, mesh=mesh, in_specs=in_specs, out_specs=out_specs, check_vma=False)
```

```python
import math

import jax
import jax.numpy as jnp
import ml_dtypes
import numpy as np
from jax import lax
from jax.experimental import pallas as pl
from jax.experimental.pallas import tpu as pltpu
from jax.sharding import PartitionSpec as P


AXES = ("scan", "cuts")
N = 256
H = 128
BF = jnp.bfloat16
F32 = jnp.float32


def dft_constants():
    k = np.arange(H)[:, None].astype(np.float64)
    j = np.arange(H)[None, :].astype(np.float64)
    even = np.exp(-2j * np.pi * j * k / H) / math.sqrt(N)
    odd = np.exp(-2j * np.pi * j * (2 * k + 1) / N) / math.sqrt(N)

    def real_form(c):
        return np.block([[c.real, -c.imag], [c.imag, c.real]])

    def parts(m):
        hi = m.astype(np.float32).astype(ml_dtypes.bfloat16)
        lo = (m - hi.astype(np.float64)).astype(np.float32).astype(ml_dtypes.bfloat16)
        return hi, lo

    e, o = real_form(even), real_form(odd)
    tables = [parts(m) for m in (e, o, e.T, o.T)]
    order = np.zeros((N, N), np.float32)
    order[np.arange(N), np.concatenate([np.arange(0, N, 2), np.arange(1, N, 2)])] = 1.0
    return np.stack([np.stack(t) for t in tables]), order


def split(x):
    hi = x.astype(BF)
    lo = (x - hi.astype(F32)).astype(BF)
    return hi, lo


def left_dot(mats, index, x):
    hi, lo = split(x)
    m = jnp.concatenate([mats[index, 0], mats[index, 0], mats[index, 1]], axis=1)
    return jnp.dot(m, jnp.concatenate([hi, lo, hi], axis=0), preferred_element_type=F32)


def right_dot(x, mats, index):
    hi, lo = split(x)
    m = jnp.concatenate([mats[index, 0], mats[index, 0], mats[index, 1]], axis=0)
    return jnp.dot(jnp.concatenate([hi, lo, hi], axis=1), m, preferred_element_type=F32)


def cat0(a, b):
    return jnp.concatenate([a, b], axis=0)


def cat1(a, b):
    return jnp.concatenate([a, b], axis=1)


def dft(re, im, mats):
    u = cat0(re[:H] + re[H:], im[:H] + im[H:])
    v = cat0(re[:H] - re[H:], im[:H] - im[H:])
    ye = left_dot(mats, 0, u)
    yo = left_dot(mats, 1, v)

    def cols(y):
        r, i = y[:H], y[H:]
        return (
            cat1(r[:, :H] + r[:, H:], i[:, :H] + i[:, H:]),
            cat1(r[:, :H] - r[:, H:], i[:, :H] - i[:, H:]),
        )

    ue, ve = cols(ye)
    uo, vo = cols(yo)
    return right_dot(cat0(ue, uo), mats, 2), right_dot(cat0(ve, vo), mats, 3)


def idft(pe, po, mats):
    e = right_dot(pe, mats, 0)
    o = right_dot(po, mats, 1)
    lt, rt = e + o, e - o
    re = cat1(lt[:, :H], rt[:, :H])
    im = cat1(lt[:, H:], rt[:, H:])
    a = left_dot(mats, 2, cat0(re[:H], im[:H]))
    b = left_dot(mats, 3, cat0(re[H:], im[H:]))
    t, w = a + b, a - b
    return cat0(t[:H], w[:H]), cat0(t[H:], w[H:])


def times_kernel(p, kr, ki, sign):
    r, i = p[:, :H], p[:, H:]
    if sign > 0:
        return cat1(r * kr - i * ki, r * ki + i * kr)
    return cat1(r * kr + i * ki, i * kr - r * ki)


def chain_body(forward, backward, meta, *refs):
    refs = list(refs)
    fixed = [refs.pop(0) for _ in range(5 if forward and backward else 4)]
    windows = [refs.pop(0) for _ in range(4)]
    old = refs.pop(0) if not forward else None
    if not forward:
        refs = refs[4:]
    wave_out = refs.pop(0)
    past_out = refs.pop(0) if not backward else None
    pieces = [refs.pop(0) for _ in range(4)] if backward else None
    w, hist, psi, out, wave_in, mats, kr, ki, target, in_sem, past_sem, out_sem, fixed_sem = refs
    plane, block, row, col = meta[0], meta[1], meta[2], meta[3]
    active = meta[5] if forward and backward else meta[4]
    slots = [
        4 * b + 2 * s + layer
        for b, s in (
            (block, plane), (block, 1 - plane), (1 - block, plane), (1 - block, 1 - plane)
        )
        for layer in range(2)
    ]

    def propagate(re, im, sign):
        pe, po = dft(re, im, mats)
        pe = times_kernel(pe, kr[:, :H], ki[:, :H], sign)
        po = times_kernel(po, kr[:, H:], ki[:, H:], sign)
        return idft(pe, po, mats)

    def past_copy(s):
        if forward:
            return pltpu.make_async_copy(hist.at[s], past_out.at[s], past_sem.at[s])
        return pltpu.make_async_copy(old.at[s], hist.at[s], past_sem.at[s])

    def wait_window(s):
        pltpu.make_async_copy(windows[0].at[:, 0], w.at[s], in_sem.at[s]).wait()

    @pl.when(active == 1)
    def _():
        for i in range(8):
            pltpu.make_async_copy(
                windows[i // 2].at[:, i % 2], w.at[slots[i]], in_sem.at[slots[i]]
            ).start()
        if not forward:
            for s in range(7, -1, -1):
                past_copy(s).start()
        for i, (source, place) in enumerate(zip(fixed, (wave_in, mats, kr, ki, target))):
            pltpu.make_async_copy(source, place, fixed_sem.at[i]).start()
        for i, (source, place) in enumerate(zip(fixed, (wave_in, mats, kr, ki, target))):
            pltpu.make_async_copy(source, place, fixed_sem.at[i]).wait()
        if forward and not backward:
            for part in range(2):
                psi[part] = pltpu.roll(pltpu.roll(wave_in[part], row, 0), col, 1)
        else:
            psi[...] = wave_in[...]

        def chi_of(s):
            wr, wi, pr, pi = w[s, 0], w[s, 1], psi[0], psi[1]
            return wr * pr - wi * pi, wr * pi + wi * pr

        def step(s, c):
            wait_window(s)
            hist[s] = psi[...]
            re, im = chi_of(s)
            re, im = propagate(re, im, 1)
            psi[0] = re
            psi[1] = im
            return c

        def emit(s, gr, gi):
            pr, pi = hist[s, 0], hist[s, 1]
            out[s, 0] = pr * gr + pi * gi
            out[s, 1] = pr * gi - pi * gr
            wr, wi = w[s, 0], w[s, 1]
            psi[0] = wr * gr + wi * gi
            psi[1] = wr * gi - wi * gr

        def piece_copy(s, i):
            return pltpu.make_async_copy(out.at[s], pieces[i // 2].at[:, i % 2], out_sem.at[i])

        def leave(s):
            for i in range(8):

                @pl.when(s == slots[i])
                def _():
                    piece_copy(s, i).start()

        def step_back(count):
            def run(q, c):
                s = count - 1 - q
                if not forward:
                    wait_window(s)
                    past_copy(s).wait()

                re, im = propagate(psi[0], psi[1], -1)
                emit(s, re, im)
                leave(s)
                return c

            return run

        if forward and not backward:

            def run(s, c):
                step(s, c)
                past_copy(s).start()
                return c

            lax.fori_loop(0, 8, run, 0)
            wave_out[...] = psi[...]
            for s in range(8):
                past_copy(s).wait()
        if forward and backward:
            lax.fori_loop(0, 7, step, 0)
            wait_window(7)
            hist[7] = psi[...]
            re, im = chi_of(7)
            pe, po = dft(re, im, mats)

            def detect(p, m):
                r, i = p[:, :H], p[:, H:]
                f = r * r + i * i - m
                return cat1(r * f, i * f)

            re, im = idft(detect(pe, target[:, :H]), detect(po, target[:, H:]), mats)
            emit(7, re, im)
            leave(7)
            lax.fori_loop(0, 7, step_back(7), 0)
            wave_out[...] = psi[...]
        if backward and not forward:
            lax.fori_loop(0, 8, step_back(8), 0)
            for part in range(2):
                undone = pltpu.roll(psi[part], lax.rem(N - row, N), 0)
                wave_out[part] = pltpu.roll(undone, lax.rem(N - col, N), 1)
        if backward:
            for i in range(8):
                piece_copy(0, i).wait()

    if not forward:

        @pl.when(active == 0)
        def _():
            wave_out[...] = jnp.zeros_like(wave_out)


def in_hbm(value):
    return pltpu.with_memory_space_constraint(value, pltpu.HBM)


def run_chain(forward, backward, meta, wave, tables, target, windows, old, pieces):
    vm = pl.BlockSpec(memory_space=pltpu.VMEM)
    hbm = pl.BlockSpec(memory_space=pl.ANY)
    far = pl.BlockSpec(memory_space=pltpu.HBM)
    operands, specs = [meta, wave, *tables], [pl.BlockSpec(memory_space=pltpu.SMEM)] + [hbm] * 4
    if forward and backward:
        operands, specs = operands + [target], specs + [hbm]
    operands, specs = operands + list(windows), specs + [hbm] * 4
    aliases = {}
    if not forward:
        operands, specs = operands + [old, *map(in_hbm, pieces)], specs + [far] * 5
        aliases = {len(operands) - 4 + i: 1 + i for i in range(4)}
    shapes, outs = [jax.ShapeDtypeStruct((2, N, N), F32)], [vm]
    if not backward:
        shapes, outs = shapes + [jax.ShapeDtypeStruct((8, 2, N, N), F32)], outs + [far]
    else:
        shapes += [pltpu.HBM((2, 2, N, N), F32)] * 4
        outs = outs + [far] * 4
    return pl.pallas_call(
        lambda *refs: chain_body(forward, backward, *refs),
        out_shape=tuple(shapes),
        in_specs=specs,
        out_specs=tuple(outs),
        input_output_aliases=aliases,
        scratch_shapes=[
            pltpu.VMEM((8, 2, N, N), F32),
            pltpu.VMEM((8, 2, N, N), F32),
            pltpu.VMEM((2, N, N), F32),
            pltpu.VMEM((8, 2, N, N), F32),
            pltpu.VMEM((2, N, N), F32),
            pltpu.VMEM((4, 2, N, N), BF),
            pltpu.VMEM((N, N), F32),
            pltpu.VMEM((N, N), F32),
            pltpu.VMEM((N, N), F32),
            pltpu.SemaphoreType.DMA((8,)),
            pltpu.SemaphoreType.DMA((8,)),
            pltpu.SemaphoreType.DMA((8,)),
            pltpu.SemaphoreType.DMA((5,)),
        ],
        compiler_params=pltpu.CompilerParams(vmem_limit_bytes=17 * 1024 * 1024),
        cost_estimate=pl.CostEstimate(
            flops=10_000_000, bytes_accessed=1024 * 1024, transcendentals=0
        ),
    )(*operands)


def shards(positions, probe, prop_phase, transmission, measured):
    scan_count = lax.axis_size("scan")
    cut_count = lax.axis_size("cuts")
    scan = lax.axis_index("scan")
    cut = lax.axis_index("cuts")
    core = scan % 2
    x, z = cut // 2, cut % 2
    half = x // 2
    hubx = jnp.where(core == 0, 1 + half, 3 * half)
    is_hub = x == hubx

    def send(value, route, where=lambda t, c: True):
        pairs = []
        for t in range(scan_count):
            for c in range(cut_count):
                if where(t, c):
                    tt, cc = route(t, c)
                    pairs.append((t * cut_count + c, (tt % scan_count) * cut_count + cc))
        return lax.ppermute(value, AXES, pairs)

    def hub_of(t, h):
        return 1 + h if t % 2 == 0 else 3 * h

    def beside(t, c):
        return t, c ^ 1

    def along(t, c):
        return t, c ^ 2

    def across(t, c):
        return t, c ^ 3

    def at_hub(t, c):
        return c // 2 == hub_of(t, c // 4)

    def off_hub(t, c):
        return not at_hub(t, c)

    def to_other_half(t, c):
        return t, 2 * hub_of(t, 1 - c // 4) + c % 2

    def next_tile(value):
        return send(value, lambda t, c: (t + 1, c))

    def previous_tile(value):
        return send(value, lambda t, c: (t - 1, c))

    edge = transmission[:, :, :, 768:]
    rim_chip = send(edge, lambda t, c: (t - 1, c), lambda t, c: t % 2 == 1)
    rim_near = send(edge, lambda t, c: (t - 1, c), lambda t, c: t % 2 == 0 and c % 2 == 1)
    rim_beside = send(
        edge, lambda t, c: (t - 1, c ^ 1), lambda t, c: t % 2 == 0 and c in (0, 6)
    )
    rim_across = send(
        edge, lambda t, c: (t - 1, c ^ 3), lambda t, c: t % 2 == 0 and c in (2, 4)
    )
    positions, edge = lax.optimization_barrier((positions, edge))

    first_is_a = (positions[0, 0] == N - 1) & (positions[1, 1] == 768)
    a_index = jnp.where(first_is_a, 0, 1)
    b_index = 1 - a_index
    left_own = positions[a_index, 1]
    top_b = positions[b_index, 0]

    rows = lax.broadcasted_iota(jnp.int32, (N, N), 0)
    columns = lax.broadcasted_iota(jnp.int32, (N, N), 1)

    packed = jnp.concatenate(
        [
            transmission[:, :, N - 1, :].reshape(-1),
            jnp.full((64,), left_own.astype(F32)),
            jnp.full((64,), top_b.astype(F32)),
        ]
    )
    packed_prev = next_tile(packed)
    row_prev = packed_prev[:4096].reshape(2, 2, 1, 1024)
    left_a = packed_prev[4096].astype(jnp.int32)
    top_prev = packed_prev[4160].astype(jnp.int32)
    target_a = send(
        measured[a_index], lambda t, c: (t + 1, c), lambda t, c: c == 2 * hub_of(t + 1, 1)
    )

    block_a = left_a // N
    shift_a = left_a % N
    block_a2 = jnp.minimum(block_a + 1, 3)

    def pick(array):
        size = (2, 2, array.shape[2], N)
        one = lax.dynamic_slice(array, (0, 0, 0, block_a * N), size)
        two = lax.dynamic_slice(array, (0, 0, 0, block_a2 * N), size)
        return jnp.where(columns[: size[2]] >= shift_a, one, two)

    window_a = jnp.where(rows == N - 1, pick(row_prev), pick(transmission))
    roll_row = jnp.where(z == 0, N - 1, top_b)
    roll_col = jnp.where(z == 0, shift_a, 0)
    mats, order = dft_constants()

    def spectral(value):
        value = jnp.dot(order, value, precision=lax.Precision.HIGHEST)
        return jnp.dot(value, order.T, precision=lax.Precision.HIGHEST)

    phase = spectral(prop_phase)
    target = spectral(jnp.where(z == 0, target_a, measured[b_index]))
    tables = (jnp.asarray(mats), jnp.cos(phase), jnp.sin(phase))
    meta = jnp.stack(
        [z, hubx % 2, roll_row, roll_col, is_hub & (half == 0), is_hub & (half == 1)]
    ).astype(jnp.int32)

    above = rows >= top_b
    give = jnp.where(z == 0, jnp.where((core == 1) | above, edge, rim_chip), window_a)
    beside_hub, across_hub = send(give, beside, at_hub), send(give, across, off_hub)
    rim_near, give, tables = lax.optimization_barrier((rim_near, give, tables))
    rim_own = jnp.where(core == 0, rim_chip, rim_near)
    keep = jnp.where(z == 0, window_a, jnp.where(above, edge, rim_own))
    along_hub = send(keep, along, off_hub)
    unmerged = (core == 1) & (z == 1) & jnp.logical_not(above)
    windows = [
        keep,
        jnp.where(unmerged, rim_beside, beside_hub),
        along_hub,
        jnp.where(unmerged, rim_across, across_hub),
    ]
    wave, past = run_chain(True, False, meta, probe, tables, None, windows, None, None)
    wave = send(wave, to_other_half, lambda t, c: c < 4 and at_hub(t, c))
    wave, *pieces = run_chain(True, True, meta, wave, tables, target, windows, None, None)
    wave = send(wave, to_other_half, lambda t, c: c >= 4 and at_hub(t, c))
    wave, *pieces = run_chain(False, True, meta, wave, tables, None, windows, past, pieces)

    spread = lax.all_to_all(wave, "cuts", 1, 1, tiled=True)
    own_rows = N // cut_count
    total = jnp.sum(spread.reshape(2, cut_count, own_rows, N), axis=1)
    total = total.reshape(2 * own_rows, N)
    total = total + send(total, lambda t, c: (t ^ 1, c), lambda t, c: t % 2 == 1)
    for stride in (2, 8):

        def turned(t, turn):
            digit = t // stride % 4
            return t + ((digit + turn) % 4 - digit) * stride

        turns = [
            send(total, lambda t, c: (turned(t, turn), c), lambda t, c: t % 2 == 0)
            for turn in (1, 2, 3)
        ]
        total = total + turns[0] + turns[1] + turns[2]
    other = send(total, lambda t, c: (t ^ 1, c), lambda t, c: t % 2 == 0)
    probe_grad = jnp.where(core == 0, total, other).reshape(2, own_rows, N)

    lent = send(pieces[1], beside, at_hub)
    kept_far = send(pieces[2], along, at_hub)
    lent_far = send(pieces[3], across, at_hub)

    kept = jnp.where(is_hub, pieces[0], kept_far)
    lent = jnp.where(is_hub, lent, lent_far)
    grad_a = jnp.where(z == 0, kept, lent)
    grad_b = jnp.where(z == 0, lent, kept)
    low = next_tile(grad_b)
    top_row = previous_tile(grad_a[:, :, N - 1 :])

    block_own = left_own // N
    shift_own = left_own % N

    def place(value, block, shift, index):
        cols = columns[: value.shape[2]]
        return jnp.where((block == index) & (cols >= shift), value, 0.0) + jnp.where(
            (block + 1 == index) & (cols < shift), value, 0.0
        )

    low_b = jnp.where(rows < top_prev, low, 0.0)
    parts = []
    for index in range(4):
        part = jnp.where(rows < N - 1, place(grad_a, block_a, shift_a, index), 0.0)
        extra = place(top_row, block_own, shift_own, index)
        part = part + jnp.where(rows == N - 1, extra, 0.0)
        if index == 3:
            part = part + jnp.where(above, grad_b, 0.0) + low_b
        parts.append(part)
    object_grad = jnp.concatenate(parts, axis=3)
    return object_grad, probe_grad


def solution(mesh):
    in_specs = (P("scan", None), P(), P(), P(None, "cuts", "scan", None), P("scan", None, None))
    out_specs = (P(None, "cuts", "scan", None), P(None, "cuts", None))
    return jax.shard_map(shards, mesh=mesh, in_specs=in_specs, out_specs=out_specs, check_vma=False)
```

```python
import math

import jax
import jax.numpy as jnp
import ml_dtypes
import numpy as np
from jax import lax
from jax.experimental import pallas as pl
from jax.experimental.pallas import tpu as pltpu
from jax.sharding import PartitionSpec as P


AXES = ("scan", "cuts")
N = 256
H = 128
BF = jnp.bfloat16
F32 = jnp.float32


def dft_constants():
    k = np.arange(H)[:, None].astype(np.float64)
    j = np.arange(H)[None, :].astype(np.float64)
    even = np.exp(-2j * np.pi * j * k / H) / math.sqrt(N)
    odd = np.exp(-2j * np.pi * j * (2 * k + 1) / N) / math.sqrt(N)

    def real_form(c):
        return np.block([[c.real, -c.imag], [c.imag, c.real]])

    def parts(m):
        hi = m.astype(np.float32).astype(ml_dtypes.bfloat16)
        lo = (m - hi.astype(np.float64)).astype(np.float32).astype(ml_dtypes.bfloat16)
        return hi, lo

    e, o = real_form(even), real_form(odd)
    tables = [parts(m) for m in (e, o, e.T, o.T)]
    order = np.zeros((N, N), np.float32)
    order[np.arange(N), np.concatenate([np.arange(0, N, 2), np.arange(1, N, 2)])] = 1.0
    return np.stack([np.stack(t) for t in tables]), order


def split(x):
    hi = x.astype(BF)
    lo = (x - hi.astype(F32)).astype(BF)
    return hi, lo


def left_dot(mats, index, x):
    hi, lo = split(x)
    m = jnp.concatenate([mats[index, 0], mats[index, 0], mats[index, 1]], axis=1)
    return jnp.dot(m, jnp.concatenate([hi, lo, hi], axis=0), preferred_element_type=F32)


def right_dot(x, mats, index):
    hi, lo = split(x)
    m = jnp.concatenate([mats[index, 0], mats[index, 0], mats[index, 1]], axis=0)
    return jnp.dot(jnp.concatenate([hi, lo, hi], axis=1), m, preferred_element_type=F32)


def cat0(a, b):
    return jnp.concatenate([a, b], axis=0)


def cat1(a, b):
    return jnp.concatenate([a, b], axis=1)


def dft(re, im, mats):
    u = cat0(re[:H] + re[H:], im[:H] + im[H:])
    v = cat0(re[:H] - re[H:], im[:H] - im[H:])
    ye = left_dot(mats, 0, u)
    yo = left_dot(mats, 1, v)

    def cols(y):
        r, i = y[:H], y[H:]
        return (
            cat1(r[:, :H] + r[:, H:], i[:, :H] + i[:, H:]),
            cat1(r[:, :H] - r[:, H:], i[:, :H] - i[:, H:]),
        )

    ue, ve = cols(ye)
    uo, vo = cols(yo)
    return right_dot(cat0(ue, uo), mats, 2), right_dot(cat0(ve, vo), mats, 3)


def idft(pe, po, mats):
    e = right_dot(pe, mats, 0)
    o = right_dot(po, mats, 1)
    lt, rt = e + o, e - o
    re = cat1(lt[:, :H], rt[:, :H])
    im = cat1(lt[:, H:], rt[:, H:])
    a = left_dot(mats, 2, cat0(re[:H], im[:H]))
    b = left_dot(mats, 3, cat0(re[H:], im[H:]))
    t, w = a + b, a - b
    return cat0(t[:H], w[:H]), cat0(t[H:], w[H:])


def times_kernel(p, kr, ki, sign):
    r, i = p[:, :H], p[:, H:]
    if sign > 0:
        return cat1(r * kr - i * ki, r * ki + i * kr)
    return cat1(r * kr + i * ki, i * kr - r * ki)


def chain_body(forward, backward, meta, *refs):
    refs = list(refs)
    fixed = [refs.pop(0) for _ in range(5 if forward and backward else 4)]
    windows = [refs.pop(0) for _ in range(4)]
    old = refs.pop(0) if not forward else None
    if not forward:
        refs = refs[4:]
    wave_out = refs.pop(0)
    past_out = refs.pop(0) if not backward else None
    pieces = [refs.pop(0) for _ in range(4)] if backward else None
    w, hist, psi, out, wave_in, mats, kr, ki, target, in_sem, past_sem, out_sem, fixed_sem = refs
    plane, block, row, col = meta[0], meta[1], meta[2], meta[3]
    active = meta[5] if forward and backward else meta[4]
    slots = [
        4 * b + 2 * s + layer
        for b, s in (
            (block, plane), (block, 1 - plane), (1 - block, plane), (1 - block, 1 - plane)
        )
        for layer in range(2)
    ]

    def propagate(re, im, sign):
        pe, po = dft(re, im, mats)
        pe = times_kernel(pe, kr[:, :H], ki[:, :H], sign)
        po = times_kernel(po, kr[:, H:], ki[:, H:], sign)
        return idft(pe, po, mats)

    def past_copy(s):
        if forward:
            return pltpu.make_async_copy(hist.at[s], past_out.at[s], past_sem.at[s])
        return pltpu.make_async_copy(old.at[s], hist.at[s], past_sem.at[s])

    def wait_window(s):
        pltpu.make_async_copy(windows[0].at[:, 0], w.at[s], in_sem.at[s]).wait()

    @pl.when(active == 1)
    def _():
        for i in range(8):
            pltpu.make_async_copy(
                windows[i // 2].at[:, i % 2], w.at[slots[i]], in_sem.at[slots[i]]
            ).start()
        if not forward:
            for s in range(7, -1, -1):
                past_copy(s).start()
        for i, (source, place) in enumerate(zip(fixed, (wave_in, mats, kr, ki, target))):
            pltpu.make_async_copy(source, place, fixed_sem.at[i]).start()
        for i, (source, place) in enumerate(zip(fixed, (wave_in, mats, kr, ki, target))):
            pltpu.make_async_copy(source, place, fixed_sem.at[i]).wait()
        if forward and not backward:
            for part in range(2):
                psi[part] = pltpu.roll(pltpu.roll(wave_in[part], row, 0), col, 1)
        else:
            psi[...] = wave_in[...]

        def chi_of(s):
            wr, wi, pr, pi = w[s, 0], w[s, 1], psi[0], psi[1]
            return wr * pr - wi * pi, wr * pi + wi * pr

        def step(s, c):
            wait_window(s)
            hist[s] = psi[...]
            re, im = chi_of(s)
            re, im = propagate(re, im, 1)
            psi[0] = re
            psi[1] = im
            return c

        def emit(s, gr, gi):
            pr, pi = hist[s, 0], hist[s, 1]
            out[s, 0] = pr * gr + pi * gi
            out[s, 1] = pr * gi - pi * gr
            wr, wi = w[s, 0], w[s, 1]
            psi[0] = wr * gr + wi * gi
            psi[1] = wr * gi - wi * gr

        def piece_copy(s, i):
            return pltpu.make_async_copy(out.at[s], pieces[i // 2].at[:, i % 2], out_sem.at[i])

        def leave(s):
            for i in range(8):

                @pl.when(s == slots[i])
                def _():
                    piece_copy(s, i).start()

        def step_back(count):
            def run(q, c):
                s = count - 1 - q
                if not forward:
                    wait_window(s)
                    past_copy(s).wait()

                re, im = propagate(psi[0], psi[1], -1)
                emit(s, re, im)
                leave(s)
                return c

            return run

        if forward and not backward:

            def run(s, c):
                step(s, c)
                past_copy(s).start()
                return c

            lax.fori_loop(0, 8, run, 0)
            wave_out[...] = psi[...]
            for s in range(8):
                past_copy(s).wait()
        if forward and backward:
            lax.fori_loop(0, 7, step, 0)
            wait_window(7)
            hist[7] = psi[...]
            re, im = chi_of(7)
            pe, po = dft(re, im, mats)

            def detect(p, m):
                r, i = p[:, :H], p[:, H:]
                f = r * r + i * i - m
                return cat1(r * f, i * f)

            re, im = idft(detect(pe, target[:, :H]), detect(po, target[:, H:]), mats)
            emit(7, re, im)
            leave(7)
            lax.fori_loop(0, 7, step_back(7), 0)
            wave_out[...] = psi[...]
        if backward and not forward:
            lax.fori_loop(0, 8, step_back(8), 0)
            for part in range(2):
                undone = pltpu.roll(psi[part], lax.rem(N - row, N), 0)
                undone = pltpu.roll(undone, lax.rem(N - col, N), 1)
                for index in range(wave_out.shape[0]):
                    size = wave_out.shape[2]
                    wave_out[index, part] = undone[index * size : (index + 1) * size]
        if backward:
            for i in range(8):
                piece_copy(0, i).wait()

    if not forward:

        @pl.when(active == 0)
        def _():
            wave_out[...] = jnp.zeros_like(wave_out)


def in_hbm(value):
    return pltpu.with_memory_space_constraint(value, pltpu.HBM)


def run_chain(forward, backward, cut_count, meta, wave, tables, target, windows, old, pieces):
    vm = pl.BlockSpec(memory_space=pltpu.VMEM)
    hbm = pl.BlockSpec(memory_space=pl.ANY)
    far = pl.BlockSpec(memory_space=pltpu.HBM)
    operands, specs = [meta, wave, *tables], [pl.BlockSpec(memory_space=pltpu.SMEM)] + [hbm] * 4
    if forward and backward:
        operands, specs = operands + [target], specs + [hbm]
    operands, specs = operands + list(windows), specs + [hbm] * 4
    aliases = {}
    if not forward:
        operands, specs = operands + [old, *map(in_hbm, pieces)], specs + [far] * 5
        aliases = {len(operands) - 4 + i: 1 + i for i in range(4)}
    wave_shape = (2, N, N) if forward else (cut_count, 2, N // cut_count, N)
    shapes, outs = [jax.ShapeDtypeStruct(wave_shape, F32)], [vm]
    if not backward:
        shapes, outs = shapes + [jax.ShapeDtypeStruct((8, 2, N, N), F32)], outs + [far]
    else:
        shapes += [pltpu.HBM((2, 2, N, N), F32)] * 4
        outs = outs + [far] * 4
    return pl.pallas_call(
        lambda *refs: chain_body(forward, backward, *refs),
        out_shape=tuple(shapes),
        in_specs=specs,
        out_specs=tuple(outs),
        input_output_aliases=aliases,
        scratch_shapes=[
            pltpu.VMEM((8, 2, N, N), F32),
            pltpu.VMEM((8, 2, N, N), F32),
            pltpu.VMEM((2, N, N), F32),
            pltpu.VMEM((8, 2, N, N), F32),
            pltpu.VMEM((2, N, N), F32),
            pltpu.VMEM((4, 2, N, N), BF),
            pltpu.VMEM((N, N), F32),
            pltpu.VMEM((N, N), F32),
            pltpu.VMEM((N, N), F32),
            pltpu.SemaphoreType.DMA((8,)),
            pltpu.SemaphoreType.DMA((8,)),
            pltpu.SemaphoreType.DMA((8,)),
            pltpu.SemaphoreType.DMA((5,)),
        ],
        compiler_params=pltpu.CompilerParams(vmem_limit_bytes=17 * 1024 * 1024),
        cost_estimate=pl.CostEstimate(
            flops=10_000_000, bytes_accessed=1024 * 1024, transcendentals=0
        ),
    )(*operands)


def shards(positions, probe, prop_phase, transmission, measured):
    scan_count = lax.axis_size("scan")
    cut_count = lax.axis_size("cuts")
    scan = lax.axis_index("scan")
    cut = lax.axis_index("cuts")
    core = scan % 2
    x, z = cut // 2, cut % 2
    half = x // 2
    hubx = jnp.where(core == 0, 1 + half, 3 * half)
    is_hub = x == hubx

    def send(value, route, where=lambda t, c: True):
        pairs = []
        for t in range(scan_count):
            for c in range(cut_count):
                if where(t, c):
                    tt, cc = route(t, c)
                    pairs.append((t * cut_count + c, (tt % scan_count) * cut_count + cc))
        return lax.ppermute(value, AXES, pairs)

    def hub_of(t, h):
        return 1 + h if t % 2 == 0 else 3 * h

    def beside(t, c):
        return t, c ^ 1

    def along(t, c):
        return t, c ^ 2

    def across(t, c):
        return t, c ^ 3

    def at_hub(t, c):
        return c // 2 == hub_of(t, c // 4)

    def off_hub(t, c):
        return not at_hub(t, c)

    def to_other_half(t, c):
        return t, 2 * hub_of(t, 1 - c // 4) + c % 2

    def next_tile(value):
        return send(value, lambda t, c: (t + 1, c))

    def previous_tile(value):
        return send(value, lambda t, c: (t - 1, c))

    edge = transmission[:, :, :, 768:]
    rim_chip = send(edge, lambda t, c: (t - 1, c), lambda t, c: t % 2 == 1)
    rim_near = send(edge, lambda t, c: (t - 1, c), lambda t, c: t % 2 == 0 and c % 2 == 1)
    rim_beside = send(
        edge, lambda t, c: (t - 1, c ^ 1), lambda t, c: t % 2 == 0 and c in (0, 6)
    )
    rim_across = send(
        edge, lambda t, c: (t - 1, c ^ 3), lambda t, c: t % 2 == 0 and c in (2, 4)
    )
    positions, edge = lax.optimization_barrier((positions, edge))

    first_is_a = (positions[0, 0] == N - 1) & (positions[1, 1] == 768)
    a_index = jnp.where(first_is_a, 0, 1)
    b_index = 1 - a_index
    left_own = positions[a_index, 1]
    top_b = positions[b_index, 0]

    rows = lax.broadcasted_iota(jnp.int32, (N, N), 0)
    columns = lax.broadcasted_iota(jnp.int32, (N, N), 1)

    packed = jnp.concatenate(
        [
            transmission[:, :, N - 1, :].reshape(-1),
            jnp.full((64,), left_own.astype(F32)),
            jnp.full((64,), top_b.astype(F32)),
        ]
    )
    packed_prev = next_tile(packed)
    row_prev = packed_prev[:4096].reshape(2, 2, 1, 1024)
    left_a = packed_prev[4096].astype(jnp.int32)
    top_prev = packed_prev[4160].astype(jnp.int32)
    target_a = send(
        measured[a_index], lambda t, c: (t + 1, c), lambda t, c: c == 2 * hub_of(t + 1, 1)
    )

    block_a = left_a // N
    shift_a = left_a % N
    block_a2 = jnp.minimum(block_a + 1, 3)

    def pick(array):
        size = (2, 2, array.shape[2], N)
        one = lax.dynamic_slice(array, (0, 0, 0, block_a * N), size)
        two = lax.dynamic_slice(array, (0, 0, 0, block_a2 * N), size)
        return jnp.where(columns[: size[2]] >= shift_a, one, two)

    window_a = jnp.where(rows == N - 1, pick(row_prev), pick(transmission))
    roll_row = jnp.where(z == 0, N - 1, top_b)
    roll_col = jnp.where(z == 0, shift_a, 0)
    mats, order = dft_constants()

    def spectral(value):
        value = jnp.dot(order, value, precision=lax.Precision.HIGHEST)
        return jnp.dot(value, order.T, precision=lax.Precision.HIGHEST)

    phase = spectral(prop_phase)
    target = spectral(jnp.where(z == 0, target_a, measured[b_index]))
    tables = (jnp.asarray(mats), jnp.cos(phase), jnp.sin(phase))
    meta = jnp.stack(
        [z, hubx % 2, roll_row, roll_col, is_hub & (half == 0), is_hub & (half == 1)]
    ).astype(jnp.int32)

    above = rows >= top_b
    give = jnp.where(z == 0, jnp.where((core == 1) | above, edge, rim_chip), window_a)
    beside_hub, across_hub = send(give, beside, at_hub), send(give, across, off_hub)
    rim_near, give, tables = lax.optimization_barrier((rim_near, give, tables))
    rim_own = jnp.where(core == 0, rim_chip, rim_near)
    keep = jnp.where(z == 0, window_a, jnp.where(above, edge, rim_own))
    along_hub = send(keep, along, off_hub)
    unmerged = (core == 1) & (z == 1) & jnp.logical_not(above)
    windows = [
        keep,
        jnp.where(unmerged, rim_beside, beside_hub),
        along_hub,
        jnp.where(unmerged, rim_across, across_hub),
    ]
    wave, past = run_chain(True, False, cut_count, meta, probe, tables, None, windows, None, None)
    wave = send(wave, to_other_half, lambda t, c: c < 4 and at_hub(t, c))
    wave, *pieces = run_chain(True, True, cut_count, meta, wave, tables, target, windows, None, None)
    wave = send(wave, to_other_half, lambda t, c: c >= 4 and at_hub(t, c))
    wave, *pieces = run_chain(
        False, True, cut_count, meta, wave, tables, None, windows, past, pieces
    )

    spread = lax.all_to_all(wave, "cuts", 0, 0, tiled=True)
    own_rows = N // cut_count
    total = jnp.sum(spread, axis=0)
    total = total.reshape(2 * own_rows, N)
    total = total + send(total, lambda t, c: (t ^ 1, c), lambda t, c: t % 2 == 1)
    for stride in (2, 8):

        def turned(t, turn):
            digit = t // stride % 4
            return t + ((digit + turn) % 4 - digit) * stride

        turns = [
            send(total, lambda t, c: (turned(t, turn), c), lambda t, c: t % 2 == 0)
            for turn in (1, 2, 3)
        ]
        total = total + turns[0] + turns[1] + turns[2]
    other = send(total, lambda t, c: (t ^ 1, c), lambda t, c: t % 2 == 0)
    probe_grad = jnp.where(core == 0, total, other).reshape(2, own_rows, N)

    lent = send(pieces[1], beside, at_hub)
    kept_far = send(pieces[2], along, at_hub)
    lent_far = send(pieces[3], across, at_hub)

    kept = jnp.where(is_hub, pieces[0], kept_far)
    lent = jnp.where(is_hub, lent, lent_far)
    grad_a = jnp.where(z == 0, kept, lent)
    grad_b = jnp.where(z == 0, lent, kept)
    low = next_tile(grad_b)
    top_row = previous_tile(grad_a[:, :, N - 1 :])

    block_own = left_own // N
    shift_own = left_own % N

    def place(value, block, shift, index):
        cols = columns[: value.shape[2]]
        return jnp.where((block == index) & (cols >= shift), value, 0.0) + jnp.where(
            (block + 1 == index) & (cols < shift), value, 0.0
        )

    low_b = jnp.where(rows < top_prev, low, 0.0)
    parts = []
    for index in range(4):
        part = jnp.where(rows < N - 1, place(grad_a, block_a, shift_a, index), 0.0)
        extra = place(top_row, block_own, shift_own, index)
        part = part + jnp.where(rows == N - 1, extra, 0.0)
        if index == 3:
            part = part + jnp.where(above, grad_b, 0.0) + low_b
        parts.append(part)
    object_grad = jnp.concatenate(parts, axis=3)
    return object_grad, probe_grad


def solution(mesh):
    in_specs = (P("scan", None), P(), P(), P(None, "cuts", "scan", None), P("scan", None, None))
    out_specs = (P(None, "cuts", "scan", None), P(None, "cuts", None))
    return jax.shard_map(shards, mesh=mesh, in_specs=in_specs, out_specs=out_specs, check_vma=False)
```
